32 devices in a mesh: seq: 8 (over z, x), head: 4 (over y, core).
Axes of the slice: x: 2, y: 2, z: 4, core: 2. Of those that a mesh axis runs over, the one named last changes fastest.
Arguments:
- query: bfloat16 [16384, 1024], P('seq', 'head'), may hold values from -9 to 9
- key: bfloat16 [16384, 1024], P('seq', 'head'), may hold values from -9 to 9
- value: bfloat16 [16384, 1024], P('seq', 'head'), may hold values from -6 to 6
- offsets: int32 [5, 16], P(None, 'head'), may hold values from 0 to 15, as said below
Outputs:
- attended: bfloat16 [16384, 1024], P('seq', 'head')
The draws below stay inside these ranges and needn't reach their ends.
Inputs may be any that keep to these rules, and one draw needn't show every extreme that they name: offsets[0, h] is 0; offsets[l, h] lies below the rate of level l: 1, 4, 4, 4, 16; at every level some head takes the largest value.
All inputs are finite; a program needn't handle non-finite values.
Results may differ from the reference program's by a relative error of at most 0.0046.
Values may be sent and summed in bfloat16 or wider, within the bound.
A program may use at most 320 MiB of HBM per device.

```python
import jax
import jax.numpy as jnp
from jax import lax

H = 16
LEVELS = 5
SEG = 512
TOK_DEV = 2048
D = 1024
TOKENS = 16384
RATE1 = 4
RATE2 = 4
RATE3 = 4
RATE4 = 16


def entries(key, salt):
    noise = jax.random.normal(jax.random.fold_in(key, salt), (TOKENS, D), jnp.float32)
    return jnp.clip(noise, -6.0, 6.0)


def draw_query(key, part):
    return entries(key, 1).astype(jnp.bfloat16)


def draw_key(key, part):
    return entries(key, 2).astype(jnp.bfloat16)


def draw_offsets(key, part):
    rates = jnp.array([1, RATE1, RATE2, RATE3, RATE4], jnp.int32)
    drawn = jax.random.randint(key, (LEVELS, H), 0, rates[:, None]).astype(jnp.int32)
    chosen = jax.random.randint(jax.random.fold_in(key, 3), (LEVELS,), 0, H).astype(jnp.int32)
    hit = jnp.arange(H, dtype=jnp.int32)[None, :] == chosen[:, None]
    return jnp.where(hit, rates[:, None] - 1, drawn).astype(jnp.int32)


def level_of(rng, shape, cuts, least, largest):
    factor_of, own = 1.0, jax.random.fold_in(rng, 6)
    for dim, parts in cuts:
        draws = jnp.exp(jax.random.uniform(jax.random.fold_in(own, dim), (parts,), jnp.float32, least / len(cuts), largest / len(cuts)))
        factor_of = factor_of * jnp.repeat(draws, shape[dim] // parts).reshape([-1 if axis == dim else 1 for axis in range(len(shape))])
    return factor_of


def bell_draw(own_key, shape, scale, limit, split=(), kind=jnp.bfloat16):
    level = level_of(own_key, shape, split, -0.22, 0.18) if split else 1.0
    entries = jax.random.normal(own_key, shape, jnp.float32) * scale * level
    return jnp.minimum(jnp.maximum(entries, -limit), limit).astype(kind)


def setup_inputs(seed: int = 0) -> dict:
    splits = jax.random.split(jax.random.key(seed), 5)
    query = draw_query(jax.random.fold_in(splits[4], 71), 0)
    key = draw_key(jax.random.fold_in(splits[4], 71), 0)
    value = bell_draw(splits[2], (TOKENS, D), 1.0, 6.0, ((0, 8), (1, 4)))
    offsets = draw_offsets(jax.random.fold_in(splits[4], 71), 0)
    return dict(query=query, key=key, value=value, offsets=offsets)


NEG = -1e30


def pick_rows(x, rate, offs):
    rows, width = x.shape
    heads = offs.shape[0]
    shaped = x.reshape(rows // rate, rate, heads, width // heads)
    index = offs.astype(jnp.int32)[None, None, :, None]
    return jnp.take_along_axis(shaped, index, axis=1)[:, 0]


def attend(query_rows, key_rows, value_rows):
    score_scale = query_rows.shape[-1] ** -0.5
    logit_scores = jnp.einsum("auc,euc->uae", query_rows.astype(jnp.float32), key_rows.astype(jnp.float32)) * score_scale
    top = jnp.max(logit_scores, axis=2, keepdims=True)
    attention_probs = jnp.exp(logit_scores - top)
    total = jnp.sum(attention_probs, axis=2)
    rounded_probs = attention_probs.astype(jnp.bfloat16).astype(jnp.float32)
    mixed_values = jnp.einsum("xjy,yxz->jxz", rounded_probs, value_rows.astype(jnp.float32))
    return mixed_values / total.T[:, :, None], (top[:, :, 0] + jnp.log(total)).T


def spread(out, lse, rate, offs):
    count, heads, size = out.shape
    hit = jnp.arange(rate)[:, None] == offs[None, :]
    full_out = jnp.where(hit[None, :, :, None], out[:, None], 0.0).reshape(count * rate, heads, size)
    full_lse = jnp.where(hit[None], lse[:, None], NEG).reshape(count * rate, heads)
    return full_out, full_lse


def level(query, key, value, offs, span, rate):
    query_rows = pick_rows(query, rate, offs)
    key_rows = pick_rows(key, rate, offs)
    value_rows = pick_rows(value, rate, offs)
    count = span // rate
    groups = query_rows.shape[0] // count

    def one(index):
        def take(a):
            return lax.dynamic_slice_in_dim(a, index * count, count, 0)
        return attend(take(query_rows), take(key_rows), take(value_rows))

    out, lse = lax.map(one, jnp.arange(groups).astype(jnp.int32))
    out = out.reshape(groups * count, out.shape[2], out.shape[3])
    lse = lse.reshape(groups * count, lse.shape[2])
    return spread(out, lse, rate, offs)


def blend(state, found):
    top, weight, acc = state
    out, lse = found
    new = jnp.maximum(top, lse)
    keep = jnp.exp(top - new)
    fresh = jnp.exp(lse - new)
    return new, weight * keep + fresh, acc * keep[:, :, None] + fresh[:, :, None] * out


def reference(query, key, value, offsets):
    spans = (SEG, TOK_DEV, 4 * TOK_DEV, TOKENS // 2, TOKENS)
    rates = (1, RATE1, RATE2, RATE3, RATE4)
    out0, lse0 = level(query, key, value, offsets[0], spans[0], rates[0])
    state = (lse0, jnp.ones(lse0.shape, jnp.float32), out0)
    for index in range(1, LEVELS):
        state = blend(state, level(query, key, value, offsets[index], spans[index], rates[index]))
    top, weight, acc = state
    return (acc / weight[:, :, None]).reshape(TOKENS, D).astype(jnp.bfloat16)
```

```python
import functools

import jax
import jax.numpy as jnp
from jax import lax
from jax.experimental import pallas as pl
from jax.experimental.pallas import tpu as pltpu
from jax.sharding import PartitionSpec as P

SEG = 512
RATE1 = 4
NEG = -1e30
LANES = 128
BF = jnp.bfloat16
F32 = jnp.float32
MESH = pl.DeviceIdType.MESH


def flip(me, i, bits):
    out = me
    for b in range(bits):
        w = 1 << b
        mine = lax.rem(lax.div(me, w), 2)
        want = lax.rem(lax.div(jnp.int32(i), w), 2)
        out = out + want * w * (1 - 2 * mine)
    return out


def half_roll(x):
    return pltpu.roll(x, LANES // 2, 1)


def tile_of(rate):
    return 16 * max(rate, 16)


def dot(a, b):
    return jnp.dot(a, b, preferred_element_type=F32)


def dot_t(a, b):
    return lax.dot_general(a, b, (((1,), (1,)), ((), ())), preferred_element_type=F32)


def attention(q, k, v_one):
    s = dot_t(q, k)
    top = jnp.max(s, axis=1, keepdims=True)
    p = jnp.exp(s - top).astype(BF)
    return dot(p, v_one), top


def kernel(cfg, q_ref, k_ref, v_ref, offs_ref, out_ref, *scratch):
    rates, counts, fars, heads, rows, width = cfg
    levels = (2, 3, 4)
    names = ("qs", "kvs", "qr", "kv", "kv1", "os", "ls", "ro", "rl")
    bufs = {}
    pos = 0
    for l in levels:
        for nm in names:
            bufs[nm, l] = scratch[pos]
            pos += 1
    (q1, k1, v1, out_l1, lse_buf, out_buf, num, tot, mx, sq, rq, skv, rkv, so, ro_s, sl, rl_s, sfar, rfar) = scratch[pos:]

    me = lax.axis_index("seq")
    hd = lax.axis_index("head")
    gbits = heads.bit_length() - 1
    mine = lax.rem(me, heads)
    nfar = max(fars.values())
    pairs = width // LANES
    scale = (width // heads) ** (-0.5)

    def dev(i):
        return (flip(me, i, gbits), hd)

    def far_dev(b):
        return (flip(me, heads << b, gbits + b + 1), hd)

    barrier = pltpu.get_barrier_semaphore()
    for i in range(1, heads):
        pl.semaphore_signal(barrier, inc=1, device_id=dev(i), device_id_type=MESH)
    for b in range(nfar):
        pl.semaphore_signal(barrier, inc=1, device_id=far_dev(b), device_id_type=MESH)

    low = lax.broadcasted_iota(jnp.int32, (1, LANES), 1) < LANES // 2
    low_f = jnp.where(low, 1.0, 0.0)
    low_b = low_f.astype(BF)
    high_b = (1.0 - low_f).astype(BF)

    def chooser(rate, tile):
        g = tile // rate
        r = lax.broadcasted_iota(jnp.int32, (g, tile), 0)
        c = lax.broadcasted_iota(jnp.int32, (g, tile), 1)
        return jnp.where((c >= r * rate) & (c < (r + 1) * rate), 1.0, 0.0).astype(BF)

    def spreader(rate, tile, copies):
        g = tile // rate
        r = lax.broadcasted_iota(jnp.int32, (tile, g), 0)
        c = lax.broadcasted_iota(jnp.int32, (tile, g), 1)
        one = jnp.where((r >= c * rate) & (r < (c + 1) * rate), 1.0, 0.0)
        return jnp.concatenate([one] * copies, axis=1).astype(BF) if copies > 1 else one.astype(BF)

    def hits(l, rate, tile):
        r = lax.broadcasted_iota(jnp.int32, (tile, width), 0) & (rate - 1)
        return r == offs_ref[l : l + 1, :]

    def halves(a, b):
        return jnp.where(low, a, half_roll(b)), jnp.where(low, half_roll(a), b)

    def picker(l, rate):
        tile = tile_of(rate)
        choose = chooser(rate, tile)
        mask = jnp.where(hits(l, rate, tile), 1.0, 0.0).astype(BF)

        def pick(ref, t):
            return dot(choose, ref[pl.ds(pl.multiple_of(t * tile, tile), tile), :] * mask)

        return pick, tile, tile // rate, rows // tile

    def pack(l):
        pick, tile, g, steps = picker(l, rates[l])
        half = steps // 2
        qs, kvs = bufs["qs", l], bufs["kvs", l]

        def body(t, _):
            qa, qb = pick(q_ref, t), pick(q_ref, t + half)
            at = pl.ds(pl.multiple_of(t * g, g), g)
            for p in range(pairs):
                cut = slice(p * LANES, (p + 1) * LANES)
                a, b = halves(qa[:, cut], qb[:, cut])
                qs[2 * p, at, :] = a.astype(BF)
                qs[2 * p + 1, at, :] = b.astype(BF)
            for u in (t, t + half):
                kk, vv = pick(k_ref, u), pick(v_ref, u)
                at2 = pl.ds(pl.multiple_of(u * g, g), g)
                for p in range(pairs):
                    cut = slice(p * LANES, (p + 1) * LANES)
                    a, b = halves(kk[:, cut], vv[:, cut])
                    kvs[2 * p, at2, :] = a.astype(BF)
                    kvs[2 * p + 1, at2, :] = b.astype(BF)
            return 0

        lax.fori_loop(0, half, body, 0)

    def copies_in(l, i):
        n = counts[l]
        to = flip(mine, i, gbits)
        a = pltpu.make_async_remote_copy(
            src_ref=bufs["kvs", l].at[to], dst_ref=bufs["kv", l].at[pl.ds(i * n, n)],
            send_sem=skv.at[l - 2, i], recv_sem=rkv.at[l - 2, i], device_id=dev(i), device_id_type=MESH)
        b = pltpu.make_async_remote_copy(
            src_ref=bufs["qs", l].at[to], dst_ref=bufs["qr", l].at[i],
            send_sem=sq.at[l - 2, i], recv_sem=rq.at[l - 2, i], device_id=dev(i), device_id_type=MESH)
        return a, b

    def copies_back(l, i, slot):
        a = pltpu.make_async_remote_copy(
            src_ref=bufs["os", l].at[i], dst_ref=bufs["ro", l].at[slot],
            send_sem=so.at[l - 2, i], recv_sem=ro_s.at[l - 2, i], device_id=dev(i), device_id_type=MESH)
        b = pltpu.make_async_remote_copy(
            src_ref=bufs["ls", l].at[i], dst_ref=bufs["rl", l].at[slot],
            send_sem=sl.at[l - 2, i], recv_sem=rl_s.at[l - 2, i], device_id=dev(i), device_id_type=MESH)
        return a, b

    def copy_far(l, b):
        n = heads * counts[l] << b
        return pltpu.make_async_remote_copy(
            src_ref=bufs["kv", l].at[pl.ds(0, n)], dst_ref=bufs["kv", l].at[pl.ds(n, n)],
            send_sem=sfar.at[l - 2, b], recv_sem=rfar.at[l - 2, b], device_id=far_dev(b), device_id_type=MESH)

    first = True
    for l in (2, 4, 3):
        pack(l)
        if first:
            pl.semaphore_wait(barrier, heads - 1 + nfar)
            first = False
        for i in range(1, heads):
            for c in copies_in(l, i):
                c.start()
        bufs["kv", l][0 : counts[l], :] = bufs["kvs", l][mine]
        bufs["qr", l][0] = bufs["qs", l][mine]

    def pair_attention(qv, kv, vv):
        o0, m0 = attention(qv * (low_b * scale).astype(BF), kv, vv * low_b + high_b)
        o1, m1 = attention(qv * (high_b * scale).astype(BF), kv, vv * high_b + low_b)
        return (
            jnp.where(low, o0, o1),
            half_roll(jnp.where(low, o1, o0)),
            jnp.where(low, m0, m1),
        )

    qt = SEG // 2

    def first_level(t, _):
        at = pl.ds(pl.multiple_of(t * qt, qt), qt)
        keys = pl.ds(pl.multiple_of(lax.div(t, SEG // qt) * SEG, SEG), SEG)
        for p in range(pairs):
            cut = slice(p * LANES, (p + 1) * LANES)
            a, b, c = pair_attention(q_ref[at, cut], k_ref[keys, cut], v_ref[keys, cut])
            num[at, cut] = a
            tot[at, cut] = b
            mx[at, cut] = c
        return 0

    lax.fori_loop(0, rows // qt, first_level, 0)

    pick, tile, g, steps = picker(1, RATE1)

    def pick_one(t, _):
        at = pl.ds(pl.multiple_of(t * g, g), g)
        for src, dst in ((q_ref, q1), (k_ref, k1), (v_ref, v1)):
            dst[at, :] = pick(src, t).astype(BF)
        return 0

    lax.fori_loop(0, steps, pick_one, 0)

    def second_level(t, _):
        at = pl.ds(pl.multiple_of(t * qt, qt), qt)
        for p in range(pairs):
            cut = slice(p * LANES, (p + 1) * LANES)
            a, b, c = pair_attention(q1[at, cut], k1[:, cut], v1[:, cut])
            out_l1[at, cut] = a / b
            lse_buf[at, cut] = c + jnp.log(b)
        return 0

    lax.fori_loop(0, rows // RATE1 // qt, second_level, 0)

    def merge(l, rate, source, last):
        tile = tile_of(rate)
        g = tile // rate
        fine = source.dtype == F32
        s_out = spreader(rate, tile, 2 if fine else 1)
        s_lse = spreader(rate, tile, 3)
        hit = hits(l, rate, tile)

        def body(t, _):
            at = pl.ds(pl.multiple_of(t * tile, tile), tile)
            pt = pl.ds(pl.multiple_of(t * g, g), g)
            o = source[pt, :]
            if fine:
                hi = o.astype(BF).astype(F32)
                o = jnp.concatenate([hi, o - hi], axis=0).astype(BF)
            e = lse_buf[pt, :]
            e0 = e.astype(BF).astype(F32)
            e1 = (e - e0).astype(BF).astype(F32)
            e2 = e - e0 - e1
            x = dot(s_out, o)
            y = dot(s_lse, jnp.concatenate([e0, e1, e2], axis=0).astype(BF))
            y = jnp.where(hit, y, NEG)
            old = mx[at, :]
            new = jnp.maximum(old, y)
            a, b = jnp.exp(old - new), jnp.exp(y - new)
            nn = num[at, :] * a + x * b
            tt = tot[at, :] * a + b
            if last:
                out_ref[at, :] = (nn / tt).astype(BF)
            else:
                num[at, :] = nn
                tot[at, :] = tt
                mx[at, :] = new
            return 0

        lax.fori_loop(0, rows // tile, body, 0)

    merge(1, RATE1, out_l1, False)

    def arrive(l):
        for i in range(1, heads):
            for c in copies_in(l, i):
                c.wait_recv()

    def work(l):
        n = counts[l]
        h = n // 2
        kv, kv1, qr, os, ls = (bufs[nm, l] for nm in ("kv", "kv1", "qr", "os", "ls"))
        kv1[...] = kv[...] * high_b + low_b

        def body(it, _):
            i = lax.rem(it + 1, heads)
            x = qr[i].astype(F32) * scale
            qa = jnp.where(low, x, 0.0).astype(BF)
            qb = jnp.where(low, half_roll(x), 0.0).astype(BF)
            if h >= LANES:
                oa, ma = attention(qa, kv[...], kv1[...])
                ob, mb = attention(qb, kv[...], kv1[...])
                o = None
            else:
                o, m = attention(jnp.concatenate([qa, qb], axis=0), kv[...], kv1[...])
                oa, ob, ma, mb = o[:h], o[h:], m[:h], m[h:]
            ya, yb = oa / half_roll(oa), ob / half_roll(ob)
            os[i] = jnp.where(low, half_roll(ya), yb).astype(BF)
            la = ma + jnp.log(jnp.where(low, oa, 1.0))
            lb = mb + jnp.log(jnp.where(low, ob, 1.0))
            parts = [la, lb]
            if n < LANES:
                parts.append(jnp.zeros((LANES - n, LANES), F32))
            ls[i] = jnp.concatenate(parts, axis=0).T[0:8, :]

            @pl.when(it < heads - 1)
            def _():
                for c in copies_back(l, i, mine):
                    c.start()

            return 0

        lax.fori_loop(0, heads, body, 0)
        bufs["ro", l][mine] = os[0]
        bufs["rl", l][mine] = ls[0]

    def unpack(l):
        n = counts[l]
        h = n // 2
        for i in range(1, heads):
            for c in copies_back(l, i, flip(mine, i, gbits)):
                c.wait_recv()
        ro, rl = bufs["ro", l], bufs["rl", l]
        for p in range(pairs):
            cut = slice(p * LANES, (p + 1) * LANES)
            a, b = halves(ro[2 * p].astype(F32), ro[2 * p + 1].astype(F32))
            out_buf[0:h, cut] = a.astype(BF)
            out_buf[h:n, cut] = b.astype(BF)
            for c in range(max(n // LANES, 1)):
                m = min(n, LANES)
                cc = slice(c * LANES, (c + 1) * LANES)
                x0 = jnp.broadcast_to(rl[2 * p, 0:1, cc], (LANES // 2, LANES))
                x1 = jnp.broadcast_to(rl[2 * p + 1, 0:1, cc], (LANES // 2, LANES))
                e = jnp.concatenate([x0, x1], axis=0).T
                lse_buf[c * m : (c + 1) * m, cut] = e[0:m]

    for l in (2, 4, 3):
        arrive(l)
        if l == 2:
            work(2)
            continue
        for b in range(fars[l]):
            c = copy_far(l, b)
            c.start()
            c.wait_recv()
        work(l)

    for l in (2, 4, 3):
        unpack(l)
        merge(l, rates[l], out_buf, l == 3)

    for l in levels:
        for i in range(1, heads):
            for c in copies_in(l, i) + copies_back(l, i, mine):
                c.wait_send()
        for b in range(fars[l]):
            copy_far(l, b).wait_send()


def per_device(places, query, key, value, offsets):
    rows, width = query.shape
    heads = offsets.shape[1]
    size = width // heads
    rate3 = RATE1 * places // 8
    rates = {2: RATE1, 3: rate3, 4: 4 * rate3}
    counts = {l: rows // r for l, r in rates.items()}
    group_bits = heads.bit_length() - 1
    bits = places.bit_length() - 1
    fars = {2: 0, 3: bits - 1 - group_bits, 4: bits - group_bits}
    spread = jnp.repeat(offsets.astype(jnp.int32), size, axis=1)
    spread = jnp.pad(spread, ((0, 8 - spread.shape[0]), (0, 0)))
    scratch = []
    for l in (2, 3, 4):
        n = counts[l]
        keys = heads * n << fars[l]
        scratch += [
            pltpu.VMEM((heads, n // 2, LANES), BF),
            pltpu.VMEM((heads, n, LANES), BF),
            pltpu.VMEM((heads, n // 2, LANES), BF),
            pltpu.VMEM((keys, LANES), BF),
            pltpu.VMEM((keys, LANES), BF),
            pltpu.VMEM((heads, n // 2, LANES), BF),
            pltpu.VMEM((heads, 8, max(n, LANES)), F32),
            pltpu.VMEM((heads, n // 2, LANES), BF),
            pltpu.VMEM((heads, 8, max(n, LANES)), F32),
        ]
    few = rows // RATE1
    scratch += [pltpu.VMEM((few, width), BF)] * 3
    scratch += [pltpu.VMEM((few, width), F32)] * 2
    scratch += [pltpu.VMEM((few, width), BF)]
    scratch += [pltpu.VMEM((rows, width), F32)] * 3
    scratch += [pltpu.SemaphoreType.DMA((3, heads))] * 8
    scratch += [pltpu.SemaphoreType.DMA((3, max(fars[4], 1)))] * 2
    cfg = (rates, counts, fars, heads, rows, width)
    return pl.pallas_call(
        functools.partial(kernel, cfg),
        out_shape=jax.ShapeDtypeStruct((rows, width), BF),
        in_specs=[pl.BlockSpec(memory_space=pltpu.VMEM)] * 4,
        out_specs=pl.BlockSpec(memory_space=pltpu.VMEM),
        scratch_shapes=scratch,
        compiler_params=pltpu.CompilerParams(
            collective_id=0, has_side_effects=True, vmem_limit_bytes=48 * 1024 * 1024
        ),
    )(query, key, value, spread)


def solution(mesh):
    return jax.shard_map(
        functools.partial(per_device, mesh.shape["seq"]),
        mesh=mesh,
        in_specs=(P("seq", "head"), P("seq", "head"), P("seq", "head"), P(None, "head")),
        out_specs=P("seq", "head"),
        check_vma=False,
    )
```

```python
import functools

import jax
import jax.numpy as jnp
from jax import lax
from jax.experimental import pallas as pl
from jax.experimental.pallas import tpu as pltpu
from jax.sharding import PartitionSpec as P

SEG = 512
RATE1 = 4
NEG = -1e30
LANES = 128
BF = jnp.bfloat16
F32 = jnp.float32
MESH = pl.DeviceIdType.MESH


def flip(me, i, bits):
    out = me
    for b in range(bits):
        w = 1 << b
        mine = lax.rem(lax.div(me, w), 2)
        want = lax.rem(lax.div(jnp.int32(i), w), 2)
        out = out + want * w * (1 - 2 * mine)
    return out


def half_roll(x):
    return pltpu.roll(x, LANES // 2, 1)


def tile_of(rate):
    return 16 * max(rate, 16)


def dot(a, b):
    return jnp.dot(a, b, preferred_element_type=F32)


def dot_t(a, b):
    return lax.dot_general(a, b, (((1,), (1,)), ((), ())), preferred_element_type=F32)


def attention(q, k, v_one):
    s = dot_t(q, k)
    top = jnp.max(s, axis=1, keepdims=True)
    p = jnp.exp(s - top).astype(BF)
    return dot(p, v_one), top


def kernel(cfg, q_hbm, k_hbm, v_hbm, offs_ref, out_ref, *scratch):
    rates, counts, fars, heads, rows, width = cfg
    levels = (2, 3, 4)
    all_rates = {1: RATE1, **rates}
    names = ("qs", "kvs", "qr", "kv", "kv1", "os", "ls", "ro", "rl", "out", "lse")
    loads = []
    bufs = {}
    pos = 0
    for l in levels:
        for nm in names:
            bufs[nm, l] = scratch[pos]
            pos += 1
    (q_ref, k_ref, v_ref, sin, q1, k1, v1, out_l1, lse_l1, num, tot, mx, sq, rq, skv, rkv, so, ro_s, sl, rl_s, sfar, rfar) = scratch[pos:]

    bufs["out", 1], bufs["lse", 1] = out_l1, lse_l1
    for x, (a, b) in enumerate(((q_hbm, q_ref), (k_hbm, k_ref), (v_hbm, v_ref))):
        loads.append(pltpu.make_async_copy(a, b, sin.at[x]))
        loads[-1].start()

    me = lax.axis_index("seq")
    hd = lax.axis_index("head")
    gbits = heads.bit_length() - 1
    mine = lax.rem(me, heads)
    nfar = max(fars.values())
    pairs = width // LANES
    scale = (width // heads) ** (-0.5)

    def dev(i):
        return (flip(me, i, gbits), hd)

    def far_dev(b):
        return (flip(me, heads << b, gbits + b + 1), hd)

    barrier = pltpu.get_barrier_semaphore()
    for i in range(1, heads):
        pl.semaphore_signal(barrier, inc=1, device_id=dev(i), device_id_type=MESH)
    for b in range(nfar):
        pl.semaphore_signal(barrier, inc=1, device_id=far_dev(b), device_id_type=MESH)

    low = lax.broadcasted_iota(jnp.int32, (1, LANES), 1) < LANES // 2
    low_f = jnp.where(low, 1.0, 0.0)
    low_b = low_f.astype(BF)
    high_b = (1.0 - low_f).astype(BF)

    def chooser(rate, tile):
        g = tile // rate
        r = lax.broadcasted_iota(jnp.int32, (g, tile), 0)
        c = lax.broadcasted_iota(jnp.int32, (g, tile), 1)
        return jnp.where((c >= r * rate) & (c < (r + 1) * rate), 1.0, 0.0).astype(BF)

    def spreader(rate, tile, copies):
        g = tile // rate
        r = lax.broadcasted_iota(jnp.int32, (tile, g), 0)
        c = lax.broadcasted_iota(jnp.int32, (tile, g), 1)
        one = jnp.where((r >= c * rate) & (r < (c + 1) * rate), 1.0, 0.0)
        return jnp.concatenate([one] * copies, axis=1).astype(BF) if copies > 1 else one.astype(BF)

    def hits(l, rate, tile):
        r = lax.broadcasted_iota(jnp.int32, (tile, width), 0) & (rate - 1)
        lane = lax.broadcasted_iota(jnp.int32, (1, width), 1)
        want = jnp.full((1, width), offs_ref[l, 0], jnp.int32)
        for h in range(1, heads):
            want = jnp.where(lane >= h * (width // heads), offs_ref[l, h], want)
        return r == want

    def halves(a, b):
        return jnp.where(low, a, half_roll(b)), jnp.where(low, half_roll(a), b)

    def picker(l, rate):
        tile = tile_of(rate)
        choose = chooser(rate, tile)
        mask = jnp.where(hits(l, rate, tile), 1.0, 0.0).astype(BF)

        def pick(ref, t):
            return dot(choose, ref[pl.ds(pl.multiple_of(t * tile, tile), tile), :] * mask)

        return pick, tile, tile // rate, rows // tile

    def pack(l):
        pick, tile, g, steps = picker(l, rates[l])
        half = steps // 2
        qs, kvs = bufs["qs", l], bufs["kvs", l]

        def body(t, _):
            qa, qb = pick(q_ref, t), pick(q_ref, t + half)
            at = pl.ds(pl.multiple_of(t * g, g), g)
            for p in range(pairs):
                cut = slice(p * LANES, (p + 1) * LANES)
                a, b = halves(qa[:, cut], qb[:, cut])
                qs[2 * p, at, :] = a.astype(BF)
                qs[2 * p + 1, at, :] = b.astype(BF)
            for u in (t, t + half):
                kk, vv = pick(k_ref, u), pick(v_ref, u)
                at2 = pl.ds(pl.multiple_of(u * g, g), g)
                for p in range(pairs):
                    cut = slice(p * LANES, (p + 1) * LANES)
                    a, b = halves(kk[:, cut], vv[:, cut])
                    kvs[2 * p, at2, :] = a.astype(BF)
                    kvs[2 * p + 1, at2, :] = b.astype(BF)
            return 0

        lax.fori_loop(0, half, body, 0)

    def copies_in(l, i):
        n = counts[l]
        to = flip(mine, i, gbits)
        a = pltpu.make_async_remote_copy(
            src_ref=bufs["kvs", l].at[to], dst_ref=bufs["kv", l].at[pl.ds(i * n, n)],
            send_sem=skv.at[l - 2, i], recv_sem=rkv.at[l - 2, i], device_id=dev(i), device_id_type=MESH)
        b = pltpu.make_async_remote_copy(
            src_ref=bufs["qs", l].at[to], dst_ref=bufs["qr", l].at[i],
            send_sem=sq.at[l - 2, i], recv_sem=rq.at[l - 2, i], device_id=dev(i), device_id_type=MESH)
        return a, b

    def copies_back(l, i, slot):
        a = pltpu.make_async_remote_copy(
            src_ref=bufs["os", l].at[i], dst_ref=bufs["ro", l].at[slot],
            send_sem=so.at[l - 2, i], recv_sem=ro_s.at[l - 2, i], device_id=dev(i), device_id_type=MESH)
        b = pltpu.make_async_remote_copy(
            src_ref=bufs["ls", l].at[i], dst_ref=bufs["rl", l].at[slot],
            send_sem=sl.at[l - 2, i], recv_sem=rl_s.at[l - 2, i], device_id=dev(i), device_id_type=MESH)
        return a, b

    def copy_far(l, b):
        n = heads * counts[l] << b
        return pltpu.make_async_remote_copy(
            src_ref=bufs["kv", l].at[pl.ds(0, n)], dst_ref=bufs["kv", l].at[pl.ds(n, n)],
            send_sem=sfar.at[l - 2, b], recv_sem=rfar.at[l - 2, b], device_id=far_dev(b), device_id_type=MESH)

    for c in loads:
        c.wait()
    first = True
    for l in (2, 4, 3):
        pack(l)
        if first:
            pl.semaphore_wait(barrier, heads - 1 + nfar)
            first = False
        for i in range(1, heads):
            for c in copies_in(l, i):
                c.start()
        bufs["kv", l][0 : counts[l], :] = bufs["kvs", l][mine]
        bufs["qr", l][0] = bufs["qs", l][mine]

    def pair_attention(qv, kv, vv):
        o0, m0 = attention(qv * (low_b * scale).astype(BF), kv, vv * low_b + high_b)
        o1, m1 = attention(qv * (high_b * scale).astype(BF), kv, vv * high_b + low_b)
        return (
            jnp.where(low, o0, o1),
            half_roll(jnp.where(low, o1, o0)),
            jnp.where(low, m0, m1),
        )

    qt = SEG

    def first_level(t, _):
        at = pl.ds(pl.multiple_of(t * qt, qt), qt)
        keys = pl.ds(pl.multiple_of(lax.div(t, SEG // qt) * SEG, SEG), SEG)
        for p in range(pairs):
            cut = slice(p * LANES, (p + 1) * LANES)
            a, b, c = pair_attention(q_ref[at, cut], k_ref[keys, cut], v_ref[keys, cut])
            num[at, cut] = a
            tot[at, cut] = b
            mx[at, cut] = c
        return 0

    lax.fori_loop(0, rows // qt, first_level, 0)

    pick, tile, g, steps = picker(1, RATE1)

    def pick_one(t, _):
        at = pl.ds(pl.multiple_of(t * g, g), g)
        for src, dst in ((q_ref, q1), (k_ref, k1), (v_ref, v1)):
            dst[at, :] = pick(src, t).astype(BF)
        return 0

    lax.fori_loop(0, steps, pick_one, 0)

    def second_level(t, _):
        at = pl.ds(pl.multiple_of(t * qt, qt), qt)
        for p in range(pairs):
            cut = slice(p * LANES, (p + 1) * LANES)
            a, b, c = pair_attention(q1[at, cut], k1[:, cut], v1[:, cut])
            out_l1[at, cut] = a / b
            lse_l1[at, cut] = c + jnp.log(b)
        return 0

    lax.fori_loop(0, rows // RATE1 // qt, second_level, 0)

    def merge(which, last):
        tile = max(tile_of(all_rates[l]) for l in which)
        fixed = {}
        for l in which:
            rate = all_rates[l]
            fine = bufs["out", l].dtype == F32
            fixed[l] = (spreader(rate, tile, 2 if fine else 1), spreader(rate, tile, 3), hits(l, rate, tile), fine)

        def body(t, _):
            at = pl.ds(pl.multiple_of(t * tile, tile), tile)
            found = []
            old = new = mx[at, :]
            for l in which:
                s_out, s_lse, hit, fine = fixed[l]
                g = tile // all_rates[l]
                pt = pl.ds(pl.multiple_of(t * g, g), g)
                o = bufs["out", l][pt, :]
                if fine:
                    hi = o.astype(BF).astype(F32)
                    o = jnp.concatenate([hi, o - hi], axis=0).astype(BF)
                e = bufs["lse", l][pt, :]
                e0 = e.astype(BF).astype(F32)
                e1 = (e - e0).astype(BF).astype(F32)
                e2 = e - e0 - e1
                x = dot(s_out, o)
                y = dot(s_lse, jnp.concatenate([e0, e1, e2], axis=0).astype(BF))
                y = jnp.where(hit, y, NEG)
                new = jnp.maximum(new, y)
                found.append((x, y))
            a = jnp.exp(old - new)
            nn, tt = num[at, :] * a, tot[at, :] * a
            for x, y in found:
                b = jnp.exp(y - new)
                nn, tt = nn + x * b, tt + b
            if last:
                out_ref[at, :] = (nn / tt).astype(BF)
            else:
                num[at, :] = nn
                tot[at, :] = tt
                mx[at, :] = new
            return 0

        lax.fori_loop(0, rows // tile, body, 0)

    merge((1,), False)

    def arrive(l):
        for i in range(1, heads):
            for c in copies_in(l, i):
                c.wait_recv()

    def work(l):
        n = counts[l]
        h = n // 2
        kv, kv1, qr, os, ls = (bufs[nm, l] for nm in ("kv", "kv1", "qr", "os", "ls"))
        kv1[...] = kv[...] * high_b + low_b

        def body(it, _):
            i = lax.rem(it + 1, heads)
            x = qr[i].astype(F32) * scale
            qa = jnp.where(low, x, 0.0).astype(BF)
            qb = jnp.where(low, half_roll(x), 0.0).astype(BF)
            o, m = attention(jnp.concatenate([qa, qb], axis=0), kv[...], kv1[...])
            oa, ob, ma, mb = o[:h], o[h:], m[:h], m[h:]
            ya, yb = oa / half_roll(oa), ob / half_roll(ob)
            os[i] = jnp.where(low, half_roll(ya), yb).astype(BF)
            la = ma + jnp.log(jnp.where(low, oa, 1.0))
            lb = mb + jnp.log(jnp.where(low, ob, 1.0))
            parts = [la, lb]
            if n < LANES:
                parts.append(jnp.zeros((LANES - n, LANES), F32))
            ls[i] = jnp.concatenate(parts, axis=0).T[0:8, :]

            @pl.when(it < heads - 1)
            def _():
                for c in copies_back(l, i, mine):
                    c.start()

            return 0

        lax.fori_loop(0, heads, body, 0)
        bufs["ro", l][mine] = os[0]
        bufs["rl", l][mine] = ls[0]

    def unpack(l):
        n = counts[l]
        h = n // 2
        for i in range(1, heads):
            for c in copies_back(l, i, flip(mine, i, gbits)):
                c.wait_recv()
        ro, rl, out_buf, lse_buf = (bufs[nm, l] for nm in ("ro", "rl", "out", "lse"))
        for p in range(pairs):
            cut = slice(p * LANES, (p + 1) * LANES)
            a, b = halves(ro[2 * p].astype(F32), ro[2 * p + 1].astype(F32))
            out_buf[0:h, cut] = a.astype(BF)
            out_buf[h:n, cut] = b.astype(BF)
            for c in range(max(n // LANES, 1)):
                m = min(n, LANES)
                cc = slice(c * LANES, (c + 1) * LANES)
                x0 = jnp.broadcast_to(rl[2 * p, 0:1, cc], (LANES // 2, LANES))
                x1 = jnp.broadcast_to(rl[2 * p + 1, 0:1, cc], (LANES // 2, LANES))
                e = jnp.concatenate([x0, x1], axis=0).T
                lse_buf[c * m : (c + 1) * m, cut] = e[0:m]

    for l in (2, 4, 3):
        arrive(l)
        if l == 2:
            work(2)
            continue
        for b in range(fars[l]):
            c = copy_far(l, b)
            c.start()
            c.wait_recv()
        work(l)

    unpack(2)
    unpack(4)
    merge((2, 4), False)
    unpack(3)
    merge((3,), True)

    for l in levels:
        for i in range(1, heads):
            for c in copies_in(l, i) + copies_back(l, i, mine):
                c.wait_send()
        for b in range(fars[l]):
            copy_far(l, b).wait_send()


def per_device(places, query, key, value, offsets):
    rows, width = query.shape
    heads = offsets.shape[1]
    size = width // heads
    rate3 = RATE1 * places // 8
    rates = {2: RATE1, 3: rate3, 4: 4 * rate3}
    counts = {l: rows // r for l, r in rates.items()}
    group_bits = heads.bit_length() - 1
    bits = places.bit_length() - 1
    fars = {2: 0, 3: bits - 1 - group_bits, 4: bits - group_bits}
    scratch = []
    for l in (2, 3, 4):
        n = counts[l]
        keys = heads * n << fars[l]
        scratch += [
            pltpu.VMEM((heads, n // 2, LANES), BF),
            pltpu.VMEM((heads, n, LANES), BF),
            pltpu.VMEM((heads, n // 2, LANES), BF),
            pltpu.VMEM((keys, LANES), BF),
            pltpu.VMEM((keys, LANES), BF),
            pltpu.VMEM((heads, n // 2, LANES), BF),
            pltpu.VMEM((heads, 8, max(n, LANES)), F32),
            pltpu.VMEM((heads, n // 2, LANES), BF),
            pltpu.VMEM((heads, 8, max(n, LANES)), F32),
            pltpu.VMEM((n, width), BF),
            pltpu.VMEM((n, width), F32),
        ]
    few = rows // RATE1
    scratch += [pltpu.VMEM((rows, width), BF)] * 3 + [pltpu.SemaphoreType.DMA((3,))]
    scratch += [pltpu.VMEM((few, width), BF)] * 3
    scratch += [pltpu.VMEM((few, width), F32)] * 2
    scratch += [pltpu.VMEM((rows, width), F32)] * 3
    scratch += [pltpu.SemaphoreType.DMA((3, heads))] * 8
    scratch += [pltpu.SemaphoreType.DMA((3, max(fars[4], 1)))] * 2
    cfg = (rates, counts, fars, heads, rows, width)
    return pl.pallas_call(
        functools.partial(kernel, cfg),
        out_shape=jax.ShapeDtypeStruct((rows, width), BF),
        in_specs=[pl.BlockSpec(memory_space=pl.ANY)] * 3 + [pl.BlockSpec(memory_space=pltpu.SMEM)],
        out_specs=pl.BlockSpec(memory_space=pltpu.VMEM),
        scratch_shapes=scratch,
        compiler_params=pltpu.CompilerParams(
            collective_id=0, has_side_effects=True, vmem_limit_bytes=48 * 1024 * 1024
        ),
    )(query, key, value, offsets)


def solution(mesh):
    return jax.shard_map(
        functools.partial(per_device, mesh.shape["seq"]),
        mesh=mesh,
        in_specs=(P("seq", "head"), P("seq", "head"), P("seq", "head"), P(None, "head")),
        out_specs=P("seq", "head"),
        check_vma=False,
    )
```
